128 devices in a mesh: gr: 8 (over y, z_lo), gc: 16 (over z_hi, x, core).
Axes of the slice: x: 4, y: 4, z: 4 (z_hi: 2, z_lo: 2; z = z_hi * 2 + z_lo), core: 2. Of those that a mesh axis runs over, the one named last changes fastest.
Arguments:
- iterate: bfloat16 [3584, 18432], P(('gr', 'gc')), may hold values from -0.3 to 0.3, as said below
Outputs:
- update: bfloat16 [3584, 18432], P(('gr', 'gc'))
The draws below stay inside these ranges and needn't reach their ends.
Inputs may be any that keep to these rules, and one draw needn't show every extreme that they name: The iterate of earlier Newton-Schulz steps, with singular values of order one.
All inputs are finite; a program needn't handle non-finite values.
Results may differ from the reference program's by a relative error of at most 0.02.
Values may be sent and summed in bfloat16 or wider, within the bound.
No kernel may reach another device: no remote copies, remote signals or barrier semaphores. Data moves between devices by JAX's collectives and lax.ppermute only.
A program may use at most 128 MiB of HBM per device.

```python
import math
import jax
import jax.numpy as jnp

M = 3584
N = 18432


def draw_iterate(key, part):
    key = jax.random.fold_in(key, 7)
    entry_scale = 1.0 / (math.sqrt(M) + math.sqrt(N))
    values = jax.random.truncated_normal(key, -6.0, 6.0, (M, N), jnp.float32)
    return (values * entry_scale).astype(jnp.bfloat16)


def setup_inputs(seed: int = 0) -> dict:
    key_list = jax.random.split(jax.random.key(seed), 2)
    iterate = draw_iterate(jax.random.fold_in(key_list[1], 71), 0)
    return {"iterate": iterate}


LINEAR_COEF = 3.4445
CUBIC_COEF = -4.775
QUINTIC_COEF = 2.0315

def reference(iterate):
    gram_matrix = jnp.dot(iterate, iterate.T, preferred_element_type=jnp.float32).astype(jnp.bfloat16)
    squared = jnp.dot(gram_matrix, gram_matrix, preferred_element_type=jnp.float32)
    poly_matrix = (CUBIC_COEF * gram_matrix.astype(jnp.float32) + QUINTIC_COEF * squared).astype(jnp.bfloat16)
    applied = jnp.dot(poly_matrix, iterate, preferred_element_type=jnp.float32)
    update_scale = 0.2 * math.sqrt(max(M, N))
    return ((LINEAR_COEF * iterate.astype(jnp.float32) + applied) * update_scale).astype(jnp.bfloat16)
```

```python
import math

import jax
import jax.numpy as jnp
from jax import lax
from jax.sharding import Mesh
from jax.sharding import PartitionSpec as P

M = 3584
N = 18432
LINEAR_COEF = 3.4445
CUBIC_COEF = -4.775
QUINTIC_COEF = 2.0315
UPDATE_SCALE = 0.2 * math.sqrt(max(M, N))

AXES = ("y", "zl", "zh", "x", "c")
SIZES = (4, 2, 2, 4, 2)
PLANE = ("zh", "zl", "x")
BAND = M // 8
PANEL = N // 16


def dot(a, b, dims):
    return lax.dot_general(a, b, (dims, ((), ())), preferred_element_type=jnp.float32)


def body(iterate):
    tile = lax.all_to_all(iterate, PLANE, split_axis=1, concat_axis=0, tiled=True)
    panel = lax.all_gather(tile, ("y", "c"), axis=0).reshape(4, M // 4, PANEL)
    partial = jnp.stack(
        [dot(tile, panel[j], ((1,), (1,))).astype(jnp.bfloat16) for j in range(4)]
    )
    pieces = lax.all_to_all(
        partial.reshape(16, BAND // 4, M // 4), PLANE, split_axis=0, concat_axis=0, tiled=True
    )
    piece = jnp.sum(pieces.astype(jnp.float32), axis=0).astype(jnp.bfloat16)
    gathered = lax.all_gather(piece, PLANE + ("c",), axis=0).reshape(4, 4, 2, BAND // 4, M // 4)
    gram = lax.dynamic_index_in_dim(gathered, lax.axis_index("c"), axis=2, keepdims=False)
    gram = gram.reshape(4, BAND, M // 4)

    def gram_times(blocks):
        return sum(dot(gram[j], blocks[j], ((1,), (0,))) for j in range(4))

    wide_tile = tile.astype(jnp.float32)
    inner = (CUBIC_COEF * wide_tile + QUINTIC_COEF * gram_times(panel)).astype(jnp.bfloat16)
    inner_panel = lax.all_gather(inner, ("y", "c"), axis=0).reshape(4, M // 4, PANEL)
    result = ((LINEAR_COEF * wide_tile + gram_times(inner_panel)) * UPDATE_SCALE).astype(
        jnp.bfloat16
    )
    return lax.all_to_all(result, PLANE, split_axis=0, concat_axis=1, tiled=True)


def solution(mesh):
    physical = Mesh(mesh.devices.reshape(SIZES), AXES)
    return jax.shard_map(
        body, mesh=physical, in_specs=P(AXES, None), out_specs=P(AXES, None), check_vma=False
    )
```

```python
import math

import jax
import jax.numpy as jnp
import numpy as np
from jax import lax
from jax.sharding import Mesh
from jax.sharding import PartitionSpec as P

M = 3584
N = 18432
LINEAR_COEF = 3.4445
CUBIC_COEF = -4.775
QUINTIC_COEF = 2.0315
UPDATE_SCALE = 0.2 * math.sqrt(max(M, N))

AXES = ("y", "zl", "zh", "x", "c")
SIZES = (4, 2, 2, 4, 2)
PLANE = ("zh", "zl", "x")
BAND = M // 8
PANEL = N // 16
NEAR_STRIP = 88
FAR_STRIP = 32


def dot(a, b, dims):
    return lax.dot_general(a, b, (dims, ((), ())), preferred_element_type=jnp.float32)


def move(a, dy=0, dc=0):
    index = np.arange(math.prod(SIZES)).reshape(SIZES)
    target = np.roll(np.roll(index, -dy, axis=0), -dc, axis=4)
    pairs = [(int(s), int(t)) for s, t in zip(index.ravel(), target.ravel())]
    return lax.ppermute(a, AXES, pairs)


def trade(a):
    return lax.all_to_all(a, PLANE, split_axis=0, concat_axis=0, tiled=True)


def forward(below, above):
    half = BAND // 2
    return move(below[:half], dy=1), move(above[half:], dy=-1)


def with_other_core(total):
    from_other = move(total[BAND:].astype(jnp.bfloat16), dc=1)
    return total[:BAND] + from_other.astype(jnp.float32)


def plane_sum(partial, rows):
    partial = jnp.pad(partial, ((0, 16 * rows - partial.shape[0]), (0, 0)))
    terms = trade(partial.reshape(16, rows, M // 4))
    return jnp.sum(terms.astype(jnp.float32), axis=0).astype(jnp.bfloat16), terms


def body(iterate):
    tile = trade(iterate.reshape(M // 128, 16, PANEL).transpose(1, 0, 2)).reshape(BAND, PANEL)
    below, above = move(tile, dy=1), move(tile, dy=-1)
    band = jnp.concatenate([tile, move(tile, dc=1)])

    def columns(rows):
        return dot(rows, band, ((1,), (1,))).astype(jnp.bfloat16)

    part, below, above = lax.optimization_barrier((columns(tile), below, above))
    far_low, far_high = forward(below, above)
    partial = jnp.concatenate([part, columns(below), columns(above)])
    strip, terms = plane_sum(partial, NEAR_STRIP)
    strip, terms, far_low, far_high = lax.optimization_barrier((strip, terms, far_low, far_high))
    gram = lax.all_gather(strip, PLANE, axis=0, tiled=True)
    far = jnp.concatenate([far_low, far_high])
    strip, _ = plane_sum(columns(far), FAR_STRIP)
    gram_far = trade(jnp.broadcast_to(strip, (16,) + strip.shape)).reshape(-1, M // 4)
    panel = jnp.concatenate([tile, below, above])
    rows = [gram[j * BAND : (j + 1) * BAND] for j in range(3)] + [gram_far[:BAND]]

    wide_tile = tile.astype(jnp.float32)
    cubed = dot(rows[3], far, ((0,), (0,))) + dot(gram[: 3 * BAND], panel, ((0,), (0,)))
    inner = CUBIC_COEF * wide_tile + QUINTIC_COEF * with_other_core(cubed)
    inner = inner.astype(jnp.bfloat16)

    below, above = move(inner, dy=1), move(inner, dy=-1)
    total, below, above = lax.optimization_barrier(
        (dot(rows[0], inner, ((0,), (0,))), below, above)
    )
    far_low, far_high = forward(below, above)
    total = total + dot(rows[1], below, ((0,), (0,))) + dot(rows[2], above, ((0,), (0,)))
    total, far_low, far_high = lax.optimization_barrier((total, far_low, far_high))
    total = total + dot(rows[3], jnp.concatenate([far_low, far_high]), ((0,), (0,)))
    update = UPDATE_SCALE * (LINEAR_COEF * wide_tile + with_other_core(total))
    update = trade(update.astype(jnp.bfloat16).reshape(16, M // 128, PANEL))
    return update.transpose(1, 0, 2).reshape(M // 128, N)


def solution(mesh):
    physical = Mesh(mesh.devices.reshape(SIZES), AXES)
    return jax.shard_map(
        body, mesh=physical, in_specs=P(AXES, None), out_specs=P(AXES, None), check_vma=False
    )
```

```python
import math

import jax
import jax.numpy as jnp
import numpy as np
from jax import lax
from jax.sharding import Mesh
from jax.sharding import PartitionSpec as P

M = 3584
N = 18432
LINEAR_COEF = 3.4445
CUBIC_COEF = -4.775
QUINTIC_COEF = 2.0315
UPDATE_SCALE = 0.2 * math.sqrt(max(M, N))

AXES = ("y", "zl", "zh", "x", "c")
SIZES = (4, 2, 2, 4, 2)
PLANE = ("zh", "zl", "x")
BAND = M // 8
PANEL = N // 16
OWN_STRIP = 32
NEAR_STRIP = 56
FAR_STRIP = 32


def dot(a, b, dims):
    return lax.dot_general(a, b, (dims, ((), ())), preferred_element_type=jnp.float32)


def move(a, dy=0, dc=0):
    index = np.arange(math.prod(SIZES)).reshape(SIZES)
    target = np.roll(np.roll(index, -dy, axis=0), -dc, axis=4)
    pairs = [(int(s), int(t)) for s, t in zip(index.ravel(), target.ravel())]
    return lax.ppermute(a, AXES, pairs)


def trade(a):
    return lax.all_to_all(a, PLANE, split_axis=0, concat_axis=0, tiled=True)


def forward(below, above):
    half = BAND // 2
    return move(below[:half], dy=1), move(above[half:], dy=-1)


def with_other_core(total):
    from_other = move(total[BAND:].astype(jnp.bfloat16), dc=1)
    return total[:BAND] + from_other.astype(jnp.float32)


def terms_of_strips(partial, rows):
    partial = jnp.pad(partial, ((0, 16 * rows - partial.shape[0]), (0, 0)))
    return trade(partial.reshape(16, rows, M // 4))


def strip_of(terms):
    return jnp.sum(terms.astype(jnp.float32), axis=0).astype(jnp.bfloat16)


def in_strips(own, below, above):
    own = jnp.pad(own, ((0, 16 * OWN_STRIP - BAND), (0, 0))).reshape(16, OWN_STRIP, PANEL)
    near = jnp.concatenate([below, above]).reshape(16, NEAR_STRIP, PANEL)
    return jnp.concatenate([own, near], axis=1).reshape(-1, PANEL)


def body(iterate):
    tile = trade(iterate.reshape(M // 128, 16, PANEL).transpose(1, 0, 2)).reshape(BAND, PANEL)
    below, above = move(tile, dy=1), move(tile, dy=-1)
    band = jnp.concatenate([tile, move(tile, dc=1)])

    def columns(rows):
        return dot(rows, band, ((1,), (1,))).astype(jnp.bfloat16)

    own_terms = terms_of_strips(columns(tile), OWN_STRIP)
    own_terms, below, above = lax.optimization_barrier((own_terms, below, above))
    far_low, far_high = forward(below, above)
    near = jnp.concatenate([columns(below), columns(above)])
    near_terms = terms_of_strips(near, NEAR_STRIP)
    near_terms, far_low, far_high = lax.optimization_barrier((near_terms, far_low, far_high))
    strip = jnp.concatenate([strip_of(own_terms), strip_of(near_terms)])
    gram = lax.all_gather(strip, PLANE, axis=0, tiled=True)
    far = jnp.concatenate([far_low, far_high])
    strip = strip_of(terms_of_strips(columns(far), FAR_STRIP))
    gram_far = trade(jnp.broadcast_to(strip, (16,) + strip.shape)).reshape(-1, M // 4)[:BAND]
    panel = in_strips(tile, below, above)

    wide_tile = tile.astype(jnp.float32)
    cubed, gram, panel = lax.optimization_barrier((dot(gram_far, far, ((0,), (0,))), gram, panel))
    cubed = cubed + dot(gram, panel, ((0,), (0,)))
    inner = CUBIC_COEF * wide_tile + QUINTIC_COEF * with_other_core(cubed)
    inner = inner.astype(jnp.bfloat16)

    below, above = move(inner, dy=1), move(inner, dy=-1)
    far_low, far_high = forward(below, above)
    total = dot(gram, in_strips(inner, below, above), ((0,), (0,)))
    total, far_low, far_high = lax.optimization_barrier((total, far_low, far_high))
    total = total + dot(gram_far, jnp.concatenate([far_low, far_high]), ((0,), (0,)))
    update = UPDATE_SCALE * (LINEAR_COEF * wide_tile + with_other_core(total))
    update = trade(update.astype(jnp.bfloat16).reshape(16, M // 128, PANEL))
    return update.transpose(1, 0, 2).reshape(M // 128, N)


def solution(mesh):
    physical = Mesh(mesh.devices.reshape(SIZES), AXES)
    return jax.shard_map(
        body, mesh=physical, in_specs=P(AXES, None), out_specs=P(AXES, None), check_vma=False
    )
```

```python
import math

import jax
import jax.numpy as jnp
import numpy as np
from jax import lax
from jax.sharding import Mesh
from jax.sharding import PartitionSpec as P

M = 3584
N = 18432
LINEAR_COEF = 3.4445
CUBIC_COEF = -4.775
QUINTIC_COEF = 2.0315
UPDATE_SCALE = 0.2 * math.sqrt(max(M, N))

AXES = ("y", "zl", "zh", "x", "c")
SIZES = (4, 2, 2, 4, 2)
PLANE = ("zh", "zl", "x")
BAND = M // 8
PANEL = N // 16
OWN_STRIP = 32
NEAR_STRIP = 56
FAR_STRIP = 32
PART = 48


def dot(a, b, dims):
    return lax.dot_general(a, b, (dims, ((), ())), preferred_element_type=jnp.float32)


def move(a, dy=0, dz=0, dx=0, dc=0):
    index = np.arange(math.prod(SIZES)).reshape(SIZES)
    by_place = index.transpose(0, 2, 1, 3, 4).reshape(4, 4, 4, 2)
    target = np.roll(by_place, (-dy, -dz, -dx, -dc), axis=(0, 1, 2, 3))
    pairs = [(int(s), int(t)) for s, t in zip(by_place.ravel(), target.ravel())]
    return lax.ppermute(a, AXES, pairs)


def gather_ring(a, axis):
    return jnp.stack([a, move(a, **{axis: -1}), move(a, **{axis: 2}), move(a, **{axis: 1})])


def trade(a):
    return lax.all_to_all(a, PLANE, split_axis=0, concat_axis=0, tiled=True)


def forward(below, above):
    half = BAND // 2
    return move(below[:half], dy=1), move(above[half:], dy=-1)


def with_other_core(total):
    from_other = move(total[BAND:].astype(jnp.bfloat16), dc=1)
    return total[:BAND] + from_other.astype(jnp.float32)


def terms_of_strips(partial, rows):
    partial = jnp.pad(partial, ((0, 16 * rows - partial.shape[0]), (0, 0)))
    return trade(partial.reshape(16, rows, M // 4))


def strip_of(terms):
    return jnp.sum(terms.astype(jnp.float32), axis=0).astype(jnp.bfloat16)


def in_strips(own, below, above):
    own = jnp.pad(own, ((0, 16 * OWN_STRIP - BAND), (0, 0))).reshape(16, OWN_STRIP, PANEL)
    near = jnp.concatenate([below, above]).reshape(16, NEAR_STRIP, PANEL)
    return jnp.concatenate([own, near], axis=1).reshape(-1, PANEL)


def body(iterate):
    tile = trade(iterate.reshape(M // 128, 16, PANEL).transpose(1, 0, 2)).reshape(BAND, PANEL)
    below, above = move(tile, dy=1), move(tile, dy=-1)
    band = jnp.concatenate([tile, move(tile, dc=1)])

    def columns(rows):
        return dot(rows, band, ((1,), (1,))).astype(jnp.bfloat16)

    own_terms = terms_of_strips(columns(tile), OWN_STRIP)
    own_terms, below, above = lax.optimization_barrier((own_terms, below, above))
    far_low, far_high = forward(below, above)
    near = jnp.concatenate([columns(below), columns(above)])
    near_terms = terms_of_strips(near, NEAR_STRIP)
    strip = jnp.concatenate([strip_of(own_terms), strip_of(near_terms)])
    strip, far_low, far_high = lax.optimization_barrier((strip, far_low, far_high))
    gram = [
        gather_ring(gather_ring(strip[:PART], "dx"), "dz"),
        gather_ring(gather_ring(strip[PART:], "dz"), "dx"),
    ]
    far = jnp.concatenate([far_low, far_high])
    strip = strip_of(terms_of_strips(columns(far), FAR_STRIP))
    gram_far = trade(jnp.broadcast_to(strip, (16,) + strip.shape)).reshape(-1, M // 4)[:BAND]
    place = (lax.axis_index(("zh", "zl")), lax.axis_index("x"))
    panel = in_strips(tile, below, above).reshape(4, 4, -1, PANEL)
    panel = jnp.roll(panel, (-place[0], -place[1]), (0, 1))
    panel = [panel[:, :, :PART].reshape(-1, PANEL)] + [
        panel[:, :, PART:].transpose(1, 0, 2, 3).reshape(-1, PANEL)
    ]

    wide_tile = tile.astype(jnp.float32)
    cubed, gram, panel = lax.optimization_barrier((dot(gram_far, far, ((0,), (0,))), gram, panel))
    for part, rows in zip(gram, panel):
        cubed = cubed + dot(part.reshape(-1, M // 4), rows, ((0,), (0,)))
    inner = CUBIC_COEF * wide_tile + QUINTIC_COEF * with_other_core(cubed)
    inner = inner.astype(jnp.bfloat16)

    below, above = move(inner, dy=1), move(inner, dy=-1)
    far_low, far_high = forward(below, above)
    gram = jnp.concatenate([gram[0], gram[1].transpose(1, 0, 2, 3)], axis=2)
    gram = jnp.roll(gram, place, (0, 1)).reshape(-1, M // 4)
    gram, below, above = lax.optimization_barrier((gram, below, above))
    total = dot(gram, in_strips(inner, below, above), ((0,), (0,)))
    total, far_low, far_high = lax.optimization_barrier((total, far_low, far_high))
    total = total + dot(gram_far, jnp.concatenate([far_low, far_high]), ((0,), (0,)))
    update = UPDATE_SCALE * (LINEAR_COEF * wide_tile + with_other_core(total))
    update = trade(update.astype(jnp.bfloat16).reshape(16, M // 128, PANEL))
    return update.transpose(1, 0, 2).reshape(M // 128, N)


def solution(mesh):
    physical = Mesh(mesh.devices.reshape(SIZES), AXES)
    return jax.shard_map(
        body, mesh=physical, in_specs=P(AXES, None), out_specs=P(AXES, None), check_vma=False
    )
```

```python
import math

import jax
import jax.numpy as jnp
import numpy as np
from jax import lax
from jax.sharding import Mesh
from jax.sharding import PartitionSpec as P

M = 3584
N = 18432
LINEAR_COEF = 3.4445
CUBIC_COEF = -4.775
QUINTIC_COEF = 2.0315
UPDATE_SCALE = 0.2 * math.sqrt(max(M, N))

AXES = ("y", "zl", "zh", "x", "c")
SIZES = (4, 2, 2, 4, 2)
PLANE = ("zh", "zl", "x")
BAND = M // 8
PANEL = N // 16
STRIP = 32


def dot(a, b, dims):
    return lax.dot_general(a, b, (dims, ((), ())), preferred_element_type=jnp.float32)


def move(a, dy=0, dz=0, dx=0, dc=0):
    index = np.arange(math.prod(SIZES)).reshape(SIZES)
    by_place = index.transpose(0, 2, 1, 3, 4).reshape(4, 4, 4, 2)
    target = np.roll(by_place, (-dy, -dz, -dx, -dc), axis=(0, 1, 2, 3))
    pairs = [(int(s), int(t)) for s, t in zip(by_place.ravel(), target.ravel())]
    return lax.ppermute(a, AXES, pairs)


def gather_ring(a, axis):
    return jnp.stack([a, move(a, **{axis: -1}), move(a, **{axis: 2}), move(a, **{axis: 1})])


def trade(a):
    return lax.all_to_all(a, PLANE, split_axis=0, concat_axis=0, tiled=True)


def forward(below, above):
    half = BAND // 2
    return move(below[:half], dy=1), move(above[half:], dy=-1)


def with_other_core(total):
    from_other = move(total[BAND:].astype(jnp.bfloat16), dc=1)
    return total[:BAND] + from_other.astype(jnp.float32)


def in_strips(rows):
    return jnp.pad(rows, ((0, 16 * STRIP - BAND), (0, 0))).reshape(16, STRIP, -1)


def plane_sum(partial):
    terms = trade(in_strips(partial)).astype(jnp.float32)
    return jnp.sum(terms, axis=0).astype(jnp.bfloat16)


def turned(strips, sign):
    place = lax.axis_index(("zh", "zl")), lax.axis_index("x")
    return jnp.roll(strips, (sign * place[0], sign * place[1]), (0, 1))


def from_here(rows):
    return turned(in_strips(rows).reshape(4, 4, STRIP, PANEL), -1)


def from_start(strips):
    return turned(strips, 1).reshape(-1, M // 4)[:BAND]


def transposed_times(gram, rows):
    return dot(gram.reshape(-1, M // 4), rows.reshape(-1, PANEL), ((0,), (0,)))


def body(iterate):
    tile = trade(iterate.reshape(M // 128, 16, PANEL).transpose(1, 0, 2)).reshape(BAND, PANEL)
    below, above = move(tile, dy=1), move(tile, dy=-1)
    band = jnp.concatenate([tile, move(tile, dc=1)])

    def columns(rows):
        return dot(rows, band, ((1,), (1,))).astype(jnp.bfloat16)

    own = plane_sum(columns(tile))
    own, below, above = lax.optimization_barrier((own, below, above))
    part, low, high = lax.optimization_barrier(
        (columns(below), below[: BAND // 2], above[BAND // 2 :])
    )
    far_low, far_high = move(low, dy=1), move(high, dy=-1)
    row = gather_ring(own, "dx")
    strip = plane_sum(part)
    strip, row, far_low, far_high = lax.optimization_barrier((strip, row, far_low, far_high))
    first = lax.broadcasted_iota(jnp.int32, strip.shape, 1) < BAND
    across = jnp.where(first, move(strip, dy=-1), move(strip, dy=-1, dc=1))
    line = gather_ring(jnp.concatenate([strip, across]), "dz")
    panel = [from_here(tile), from_here(below).transpose(1, 0, 2, 3)]
    far = jnp.concatenate([far_low, far_high])
    strip = plane_sum(columns(far))
    strip, line, row, panel = lax.optimization_barrier((strip, line, row, panel))
    gram_far = gather_ring(gather_ring(strip, "dx"), "dz")
    lines = gather_ring(line, "dx")
    gram_own = gather_ring(row, "dz")
    gram_below = lines[:, :, :STRIP]
    gram_above = from_start(lines[:, :, STRIP:].transpose(1, 0, 2, 3))
    gram_above = jnp.concatenate([gram_above[:, :BAND], gram_above[:, BAND:]])

    wide_tile = tile.astype(jnp.float32)
    cubed = transposed_times(gram_own, panel[0]) + transposed_times(gram_far, from_here(far))
    cubed = cubed + transposed_times(gram_below, panel[1])
    cubed = cubed + dot(gram_above, above, ((1,), (0,)))
    inner = CUBIC_COEF * wide_tile + QUINTIC_COEF * with_other_core(cubed)
    inner = inner.astype(jnp.bfloat16)

    below, above = move(inner, dy=1), move(inner, dy=-1)
    far_low, far_high = forward(below, above)
    gram_own, gram_far = from_start(gram_own), from_start(gram_far)
    gram_below = from_start(gram_below.transpose(1, 0, 2, 3))
    total = transposed_times(gram_own, inner)
    total, gram_below, gram_far, below, above = lax.optimization_barrier(
        (total, gram_below, gram_far, below, above)
    )
    total = total + transposed_times(gram_below, below) + dot(gram_above, above, ((1,), (0,)))
    total, far_low, far_high = lax.optimization_barrier((total, far_low, far_high))
    total = total + transposed_times(gram_far, jnp.concatenate([far_low, far_high]))
    update = UPDATE_SCALE * (LINEAR_COEF * wide_tile + with_other_core(total))
    update = trade(update.astype(jnp.bfloat16).reshape(16, M // 128, PANEL))
    return update.transpose(1, 0, 2).reshape(M // 128, N)


def solution(mesh):
    physical = Mesh(mesh.devices.reshape(SIZES), AXES)
    return jax.shard_map(
        body, mesh=physical, in_specs=P(AXES, None), out_specs=P(AXES, None), check_vma=False
    )
```

```python
import math

import jax
import jax.numpy as jnp
import numpy as np
from jax import lax
from jax.sharding import Mesh
from jax.sharding import PartitionSpec as P

M = 3584
N = 18432
LINEAR_COEF = 3.4445
CUBIC_COEF = -4.775
QUINTIC_COEF = 2.0315
UPDATE_SCALE = 0.2 * math.sqrt(max(M, N))

AXES = ("y", "zl", "zh", "x", "c")
SIZES = (4, 2, 2, 4, 2)
PLANE = ("zh", "zl", "x")
BAND = M // 8
PANEL = N // 16
STRIP = 32


def dot(a, b, dims):
    return lax.dot_general(a, b, (dims, ((), ())), preferred_element_type=jnp.float32)


def move(a, dy=0, dz=0, dx=0, dc=0):
    index = np.arange(math.prod(SIZES)).reshape(SIZES)
    by_place = index.transpose(0, 2, 1, 3, 4).reshape(4, 4, 4, 2)
    target = np.roll(by_place, (-dy, -dz, -dx, -dc), axis=(0, 1, 2, 3))
    pairs = [(int(s), int(t)) for s, t in zip(by_place.ravel(), target.ravel())]
    return lax.ppermute(a, AXES, pairs)


def gather_ring(a, axis):
    return jnp.stack([a, move(a, **{axis: -1}), move(a, **{axis: 2}), move(a, **{axis: 1})])


def trade(a):
    return lax.all_to_all(a, PLANE, split_axis=0, concat_axis=0, tiled=True)


def forward(below, above):
    half = BAND // 2
    return move(below[:half], dy=1), move(above[half:], dy=-1)


def with_other_core(total):
    from_other = move(total[BAND:].astype(jnp.bfloat16), dc=1)
    return total[:BAND] + from_other.astype(jnp.float32)


def in_strips(rows):
    return jnp.pad(rows, ((0, 16 * STRIP - BAND), (0, 0))).reshape(16, STRIP, -1)


def plane_sum(partial):
    terms = trade(in_strips(partial)).astype(jnp.float32)
    return jnp.sum(terms, axis=0).astype(jnp.bfloat16)


def turned(strips, sign):
    place = lax.axis_index(("zh", "zl")), lax.axis_index("x")
    return jnp.roll(strips, (sign * place[0], sign * place[1]), (0, 1))


def from_here(rows):
    return turned(in_strips(rows).reshape(4, 4, STRIP, PANEL), -1)


def from_start(strips):
    return turned(strips, 1).reshape(-1, M // 4)[:BAND]


def transposed_times(gram, rows):
    return dot(gram.reshape(-1, M // 4), rows.reshape(-1, PANEL), ((0,), (0,)))


def body(iterate):
    tile = trade(iterate.reshape(M // 128, 16, PANEL).transpose(1, 0, 2)).reshape(BAND, PANEL)
    below, above = move(tile, dy=1), move(tile, dy=-1)
    band = jnp.concatenate([tile, move(tile, dc=1)])

    def columns(rows):
        return dot(rows, band, ((1,), (1,))).astype(jnp.bfloat16)

    own = plane_sum(columns(tile))
    own, below, above = lax.optimization_barrier((own, below, above))
    part, low, high = lax.optimization_barrier(
        (columns(below), below[: BAND // 2], above[BAND // 2 :])
    )
    far_low, far_high = move(low, dy=1), move(high, dy=-1)
    row = gather_ring(own, "dx")
    strip = plane_sum(part)
    strip, row, far_low, far_high = lax.optimization_barrier((strip, row, far_low, far_high))
    first = lax.broadcasted_iota(jnp.int32, strip.shape, 1) < BAND
    across = jnp.where(first, move(strip, dy=-1), move(strip, dy=-1, dc=1))
    line = gather_ring(jnp.concatenate([strip, across]), "dz")
    panel = [from_here(tile), from_here(below).transpose(1, 0, 2, 3)]
    far = jnp.concatenate([far_low, far_high])
    strip = plane_sum(columns(far))
    strip, line, row = lax.optimization_barrier((strip, line, row))
    gram_far = gather_ring(gather_ring(strip, "dx"), "dz")
    lines = gather_ring(line, "dx")
    gram_own = gather_ring(row, "dz")
    gram_below = lines[:, :, :STRIP]
    gram_above = from_start(lines[:, :, STRIP:].transpose(1, 0, 2, 3))
    gram_above = jnp.concatenate([gram_above[:, :BAND], gram_above[:, BAND:]])

    wide_tile = tile.astype(jnp.float32)
    cubed = transposed_times(gram_own, panel[0]) + transposed_times(gram_far, from_here(far))
    cubed = cubed + transposed_times(gram_below, panel[1])
    cubed = cubed + dot(gram_above, above, ((1,), (0,)))
    inner = CUBIC_COEF * wide_tile + QUINTIC_COEF * with_other_core(cubed)
    inner = inner.astype(jnp.bfloat16)

    below, above = move(inner, dy=1), move(inner, dy=-1)
    far_low, far_high = forward(below, above)
    gram_own, gram_far = from_start(gram_own), from_start(gram_far)
    gram_below = from_start(gram_below.transpose(1, 0, 2, 3))
    total = transposed_times(gram_own, inner)
    total, gram_below, gram_far, below, above = lax.optimization_barrier(
        (total, gram_below, gram_far, below, above)
    )
    total = total + transposed_times(gram_below, below) + dot(gram_above, above, ((1,), (0,)))
    total, far_low, far_high = lax.optimization_barrier((total, far_low, far_high))
    total = total + transposed_times(gram_far, jnp.concatenate([far_low, far_high]))
    update = UPDATE_SCALE * (LINEAR_COEF * wide_tile + with_other_core(total))
    update = trade(update.astype(jnp.bfloat16).reshape(16, M // 128, PANEL))
    return update.transpose(1, 0, 2).reshape(M // 128, N)


def solution(mesh):
    physical = Mesh(mesh.devices.reshape(SIZES), AXES)
    return jax.shard_map(
        body, mesh=physical, in_specs=P(AXES, None), out_specs=P(AXES, None), check_vma=False
    )
```
